32 devices in a mesh: clips: 2 (over y), pix: 4 (over z), pair: 2 (over x), dir: 2 (over core).
Axes of the slice: x: 2, y: 2, z: 4, core: 2. Of those that a mesh axis runs over, the one named last changes fastest.
Arguments:
- features: bfloat16 [4, 2, 1920, 128], P(('clips', 'pair'), 'dir', 'pix'), parts along dimension 0, may hold values from -6 to 6
Outputs:
- flow: float32 [4, 2, 2, 1920], P(('clips', 'pair'), 'dir', None, 'pix'), parts along dimension 0
- matched: bfloat16 [4, 2, 1920, 128], P(('clips', 'pair'), 'dir', 'pix'), parts along dimension 0
The draws below stay inside these ranges and needn't reach their ends.
There are 2 independent parts, one for each index of `clips`. The reference program is written for one: setup_inputs(seed, part) draws one part's arguments, and reference() takes and returns one part's arrays. A program takes and returns all parts, laid end to end along the dimension named above; each array names one. Nothing has to cross between parts.
All inputs are finite; a program needn't handle non-finite values.
Results may differ from the reference program's by a relative error of at most 0.0065.
Values may be sent and summed in bfloat16 or wider, within the bound.
A program may use at most 64 MiB of HBM per device.

```python
import jax
import jax.numpy as jnp
from jax import lax

C = 128
W = 120
ROWS_DEV = 4
PIXELS = 1920
PAIRS = 2


def draw_features(key, part):
    keys = jax.random.split(key, 1)
    shape = (PAIRS, 2, PIXELS, C)
    base = jnp.clip(1.75 * jax.random.normal(keys[0], shape, jnp.float32), -6.0, 6.0)
    return base.astype(jnp.bfloat16)


def setup_inputs(seed: int = 0, part: int = 0) -> dict:
    seeds = jax.random.split(jax.random.key(seed), 2)
    part_splits = jax.random.split(jax.random.fold_in(seeds[1], part), 2)
    return {
        "features": draw_features(jax.random.fold_in(jax.random.fold_in(seeds[1], part), 71), part),
    }


def match_block(queries, targets, posx, posy, own_x, own_y):
    scores = jnp.dot(queries, targets.T, preferred_element_type=jnp.float32) * (C ** -0.5)
    top = jnp.max(scores, axis=1, keepdims=True)
    weights = jnp.exp(scores - top)
    total = jnp.sum(weights, axis=1)
    flow_x = jnp.sum(weights * posx[None, :], axis=1) / total - own_x
    flow_y = jnp.sum(weights * posy[None, :], axis=1) / total - own_y
    rounded = weights.astype(jnp.bfloat16)
    summed = jnp.dot(rounded, targets, preferred_element_type=jnp.float32)
    matched = (summed / total[:, None]).astype(jnp.bfloat16)
    return jnp.stack([flow_x, flow_y]), matched


def reference(features):
    index = jnp.arange(PIXELS, dtype=jnp.int32)
    posx = (index % W).astype(jnp.float32) / W
    posy = (index // W).astype(jnp.float32) / W
    block = ROWS_DEV * W
    count = PIXELS // block
    flows = []
    matches = []
    for pair_index in range(PAIRS):
        flow_dirs = []
        match_dirs = []
        for side in range(2):
            sources = features[pair_index, side].reshape(count, block, C)
            targets = features[pair_index, 1 - side]
            own_x = posx.reshape(count, block)
            own_y = posy.reshape(count, block)

            def one_block(item):
                return match_block(item[0], targets, posx, posy, item[1], item[2])

            flow_part, match_part = lax.map(one_block, (sources, own_x, own_y))
            flow_dirs.append(jnp.transpose(flow_part, (1, 0, 2)).reshape(2, PIXELS))
            match_dirs.append(match_part.reshape(PIXELS, C))
        flows.append(jnp.stack(flow_dirs))
        matches.append(jnp.stack(match_dirs))
    return jnp.stack(flows), jnp.stack(matches)
```

```python
import functools
import math

import jax
import jax.numpy as jnp
from jax import lax
from jax.experimental import pallas as pl
from jax.experimental.pallas import tpu as pltpu
from jax.sharding import PartitionSpec as P

W = 120
LOWEST = -1e30
PARTS = 2
WIDTH = 512
SUMS = 16
LIMIT = 40 * 2**20
MESH = pl.DeviceIdType.MESH


def grid_position(index):
    row = jnp.floor((index + 0.5) * (1.0 / W))
    return index - row * W, row


def kernel(
    count, feats, flow, matched, queries, held, places, top, acc, own_sem, pass_sem, recv_sem, load_sem
):
    rows, chans = feats.shape[2], feats.shape[3]
    part = rows // PARTS
    scale = math.log2(math.e) / math.sqrt(chans)
    here = lax.axis_index("pix")
    side = lax.axis_index("dir")
    other = 1 - side
    has_left = here > 0
    has_right = here < count - 1

    load = pltpu.make_async_copy(feats.at[0, 0], queries, load_sem)
    load.start()

    barrier = pltpu.get_barrier_semaphore()

    def greet(pix, core):
        pl.semaphore_signal(
            barrier, inc=1, device_id={"pix": pix, "dir": core}, device_id_type=MESH
        )

    greet(here, other)

    @pl.when(has_left)
    def _():
        greet(here - 1, other)
        greet(here - 1, side)

    @pl.when(has_right)
    def _():
        greet(here + 1, other)
        greet(here + 1, side)

    neighbours = has_left.astype(jnp.int32) + has_right.astype(jnp.int32)
    pl.semaphore_wait(barrier, 1 + 2 * neighbours)

    def own_copy(which, pix, piece):
        span = pl.ds(piece * part, part)
        return pltpu.make_async_remote_copy(
            src_ref=feats.at[0, 0, span],
            dst_ref=held.at[here, span],
            send_sem=own_sem.at[which, piece],
            recv_sem=recv_sem.at[here, piece],
            device_id={"pix": pix, "dir": other},
            device_id_type=MESH,
        )

    def pass_copy(slot, pix, piece):
        span = pl.ds(piece * part, part)
        return pltpu.make_async_remote_copy(
            src_ref=held.at[slot, span],
            dst_ref=held.at[slot, span],
            send_sem=pass_sem.at[slot, piece],
            recv_sem=recv_sem.at[slot, piece],
            device_id={"pix": pix, "dir": side},
            device_id_type=MESH,
        )

    for piece in range(PARTS):

        @pl.when(has_left)
        def _():
            own_copy(1, here - 1, piece).start()

        @pl.when(has_right)
        def _():
            own_copy(2, here + 1, piece).start()

    for piece in range(PARTS):
        own_copy(0, here, piece).start()

    line = lax.broadcasted_iota(jnp.int32, (SUMS, rows), 0)
    local = lax.broadcasted_iota(jnp.int32, (SUMS, rows), 1)

    @pl.loop(0, count)
    def _(slot):
        col, row = grid_position((local + slot * rows).astype(jnp.float32))
        tags = jnp.where(line == 0, 1.0, jnp.where(line == 1, col, jnp.where(line == 2, row, 0.0)))
        places[slot] = tags.astype(jnp.bfloat16)

    top[...] = jnp.full_like(top, LOWEST)
    acc[...] = jnp.zeros_like(acc)
    load.wait()

    short = jnp.minimum(here, count - 1 - here)
    long_left = here > count - 1 - here

    def slot_of(item):
        paired = item <= 2 * short
        step = jnp.where(paired, (item + 1) // 2, item - short)
        left = jnp.where(paired, item % 2 == 1, long_left)
        return jnp.where(left, here - step, here + step)

    def arrive(slot, piece):
        pass_copy(slot, here, piece).wait_recv()

        @pl.when((slot < here) & has_right)
        def _():
            pass_copy(slot, here + 1, piece).start()

        @pl.when((slot > here) & has_left)
        def _():
            pass_copy(slot, here - 1, piece).start()

    def fold(slot):
        keys = held[slot]
        values = jnp.concatenate([keys.T, places[slot]], axis=0)
        for start in range(0, rows, WIDTH):
            some = slice(start, min(start + WIDTH, rows))
            scores = lax.dot_general(
                keys, queries[some], (((1,), (1,)), ((), ())), preferred_element_type=jnp.float32
            )
            old = top[:, some]
            new = jnp.maximum(old, jnp.max(scores, axis=0, keepdims=True))
            fade = jnp.exp2((old - new) * scale)
            weights = jnp.exp2((scores - new) * scale).astype(jnp.bfloat16)
            top[:, some] = new
            acc[:, some] = acc[:, some] * fade + jnp.dot(
                values, weights, preferred_element_type=jnp.float32
            )

    @pl.loop(0, count)
    def _(item):
        slot = slot_of(item)
        opens = (item % 2 == 1) & (item < 2 * short)
        second = (item > 0) & (item % 2 == 0) & (item <= 2 * short)
        for piece in range(PARTS):

            @pl.when(jnp.logical_not(second))
            def _():
                arrive(slot, piece)

            @pl.when(opens)
            def _():
                arrive(slot_of(item + 1), piece)

        fold(slot)

    inverse = 1.0 / acc[chans : chans + 1]
    matched[0, 0] = (acc[:chans] * inverse).T.astype(matched.dtype)
    means = acc[chans : chans + 8] * inverse
    index = (lax.broadcasted_iota(jnp.int32, (1, rows), 1) + here * rows).astype(jnp.float32)
    col, row = grid_position(index)
    flow[0, 0, 0:1] = (means[1:2] - col) * (1.0 / W)
    flow[0, 0, 1:2] = (means[2:3] - row) * (1.0 / W)

    for piece in range(PARTS):
        own_copy(0, here, piece).wait_send()

        @pl.when(has_left)
        def _():
            own_copy(1, here - 1, piece).wait_send()

        @pl.when(has_right)
        def _():
            own_copy(2, here + 1, piece).wait_send()

    @pl.loop(0, count)
    def _(slot):
        sent = ((slot < here) & has_right) | ((slot > here) & has_left)

        @pl.when(sent)
        def _():
            for piece in range(PARTS):
                pass_copy(slot, here, piece).wait_send()


def write_out(flow_in, matched_in, flow, matched, flow_sem, matched_sem):
    flow_copy = pltpu.make_async_copy(flow_in, flow, flow_sem)
    matched_copy = pltpu.make_async_copy(matched_in, matched, matched_sem)
    matched_copy.start()
    flow_copy.start()
    matched_copy.wait()
    flow_copy.wait()


def body(count, features):
    rows, chans = features.shape[2], features.shape[3]
    shapes = (
        jax.ShapeDtypeStruct((1, 1, 2, rows), jnp.float32),
        jax.ShapeDtypeStruct((1, 1, rows, chans), jnp.bfloat16),
    )
    flow, matched = pl.pallas_call(
        functools.partial(kernel, count),
        out_shape=shapes,
        in_specs=[pl.BlockSpec(memory_space=pl.ANY)],
        out_specs=(
            pl.BlockSpec(memory_space=pltpu.VMEM),
            pl.BlockSpec(memory_space=pltpu.VMEM),
        ),
        scratch_shapes=[
            pltpu.VMEM((rows, chans), jnp.bfloat16),
            pltpu.VMEM((count, rows, chans), jnp.bfloat16),
            pltpu.VMEM((count, SUMS, rows), jnp.bfloat16),
            pltpu.VMEM((1, rows), jnp.float32),
            pltpu.VMEM((chans + SUMS, rows), jnp.float32),
            pltpu.SemaphoreType.DMA((3, PARTS)),
            pltpu.SemaphoreType.DMA((count, PARTS)),
            pltpu.SemaphoreType.DMA((count, PARTS)),
            pltpu.SemaphoreType.DMA,
        ],
        compiler_params=pltpu.CompilerParams(
            collective_id=0, has_side_effects=True, vmem_limit_bytes=LIMIT
        ),
    )(features)
    return pl.pallas_call(
        write_out,
        out_shape=shapes,
        in_specs=[pl.BlockSpec(memory_space=pl.ANY)] * 2,
        out_specs=[pl.BlockSpec(memory_space=pl.ANY)] * 2,
        scratch_shapes=[pltpu.SemaphoreType.DMA, pltpu.SemaphoreType.DMA],
        compiler_params=pltpu.CompilerParams(vmem_limit_bytes=2**20),
    )(flow, matched)


def solution(mesh):
    placed = (P(("clips", "pair"), "dir", "pix", None),)
    return jax.shard_map(
        functools.partial(body, mesh.shape["pix"]),
        mesh=mesh,
        in_specs=placed,
        out_specs=(
            P(("clips", "pair"), "dir", None, "pix"),
            P(("clips", "pair"), "dir", "pix", None),
        ),
        check_vma=False,
    )
```

```python
import functools
import math

import jax
import jax.numpy as jnp
from jax import lax
from jax.experimental import pallas as pl
from jax.experimental.pallas import tpu as pltpu
from jax.sharding import PartitionSpec as P

W = 120
LOWEST = -1e30
PARTS = 2
WIDTH = 512
SUMS = 16
LIMIT = 40 * 2**20
MESH = pl.DeviceIdType.MESH


def grid_position(index):
    row = jnp.floor((index + 0.5) * (1.0 / W))
    return index - row * W, row


def kernel(
    count, feats, flow, matched, queries, held, places, top, acc, own_sem, pass_sem, recv_sem, load_sem
):
    rows, chans = feats.shape[2], feats.shape[3]
    part = rows // PARTS
    scale = math.log2(math.e) / math.sqrt(chans)
    here = lax.axis_index("pix")
    side = lax.axis_index("dir")
    other = 1 - side
    has_left = here > 0
    has_right = here < count - 1

    load = pltpu.make_async_copy(feats.at[0, 0], queries, load_sem)
    load.start()

    barrier = pltpu.get_barrier_semaphore()

    def greet(pix, core):
        pl.semaphore_signal(
            barrier, inc=1, device_id={"pix": pix, "dir": core}, device_id_type=MESH
        )

    greet(here, other)

    @pl.when(has_left)
    def _():
        greet(here - 1, other)
        greet(here - 1, side)

    @pl.when(has_right)
    def _():
        greet(here + 1, other)
        greet(here + 1, side)

    neighbours = has_left.astype(jnp.int32) + has_right.astype(jnp.int32)
    pl.semaphore_wait(barrier, 1 + 2 * neighbours)

    def own_copy(which, pix, piece):
        span = pl.ds(piece * part, part)
        return pltpu.make_async_remote_copy(
            src_ref=feats.at[0, 0, span],
            dst_ref=held.at[here, span],
            send_sem=own_sem.at[which, piece],
            recv_sem=recv_sem.at[here, piece],
            device_id={"pix": pix, "dir": other},
            device_id_type=MESH,
        )

    def pass_copy(slot, pix, piece):
        span = pl.ds(piece * part, part)
        return pltpu.make_async_remote_copy(
            src_ref=held.at[slot, span],
            dst_ref=held.at[slot, span],
            send_sem=pass_sem.at[slot, piece],
            recv_sem=recv_sem.at[slot, piece],
            device_id={"pix": pix, "dir": side},
            device_id_type=MESH,
        )

    for piece in range(PARTS):

        @pl.when(has_left)
        def _():
            own_copy(1, here - 1, piece).start()

        @pl.when(has_right)
        def _():
            own_copy(2, here + 1, piece).start()

    for piece in range(PARTS):
        own_copy(0, here, piece).start()

    line = lax.broadcasted_iota(jnp.int32, (SUMS, rows), 0)
    local = lax.broadcasted_iota(jnp.int32, (SUMS, rows), 1)

    @pl.loop(0, count)
    def _(slot):
        col, row = grid_position((local + slot * rows).astype(jnp.float32))
        tags = jnp.where(line == 0, 1.0, jnp.where(line == 1, col, jnp.where(line == 2, row, 0.0)))
        places[slot] = tags.astype(jnp.bfloat16)

    top[...] = jnp.full_like(top, LOWEST)
    acc[...] = jnp.zeros_like(acc)
    load.wait()

    short = jnp.minimum(here, count - 1 - here)
    long_left = here > count - 1 - here

    def slot_of(item):
        paired = item <= 2 * short
        step = jnp.where(paired, (item + 1) // 2, item - short)
        left = jnp.where(paired, item % 2 == 1, long_left)
        return jnp.where(left, here - step, here + step)

    def arrive(slot, piece):
        pass_copy(slot, here, piece).wait_recv()

        @pl.when((slot < here) & has_right)
        def _():
            pass_copy(slot, here + 1, piece).start()

        @pl.when((slot > here) & has_left)
        def _():
            pass_copy(slot, here - 1, piece).start()

    def fold(slot, first, length):
        keys = held[slot, first : first + length]
        values = jnp.concatenate([keys.T, places[slot, :, first : first + length]], axis=0)
        for start in range(0, rows, WIDTH):
            some = slice(start, min(start + WIDTH, rows))
            scores = lax.dot_general(
                keys, queries[some], (((1,), (1,)), ((), ())), preferred_element_type=jnp.float32
            )
            old = top[:, some]
            new = jnp.maximum(old, jnp.max(scores, axis=0, keepdims=True))
            fade = jnp.exp2((old - new) * scale)
            weights = jnp.exp2((scores - new) * scale).astype(jnp.bfloat16)
            top[:, some] = new
            acc[:, some] = acc[:, some] * fade + jnp.dot(
                values, weights, preferred_element_type=jnp.float32
            )

    @pl.loop(0, count - 1)
    def _(item):
        slot = slot_of(item)
        opens = (item % 2 == 1) & (item < 2 * short)
        second = (item > 0) & (item % 2 == 0) & (item <= 2 * short)
        for piece in range(PARTS):

            @pl.when(jnp.logical_not(second))
            def _():
                arrive(slot, piece)

            @pl.when(opens)
            def _():
                arrive(slot_of(item + 1), piece)

        fold(slot, 0, rows)

    final = slot_of(count - 1)
    for piece in range(PARTS):

        @pl.when((here == 0) | (here == count - 1) | (count > 2 * short + 1))
        def _():
            arrive(final, piece)

        fold(final, piece * part, part)

    inverse = 1.0 / acc[chans : chans + 1]
    matched[0, 0] = (acc[:chans] * inverse).T.astype(matched.dtype)
    means = acc[chans : chans + 8] * inverse
    index = (lax.broadcasted_iota(jnp.int32, (1, rows), 1) + here * rows).astype(jnp.float32)
    col, row = grid_position(index)
    flow[0, 0, 0:1] = (means[1:2] - col) * (1.0 / W)
    flow[0, 0, 1:2] = (means[2:3] - row) * (1.0 / W)

    for piece in range(PARTS):
        own_copy(0, here, piece).wait_send()

        @pl.when(has_left)
        def _():
            own_copy(1, here - 1, piece).wait_send()

        @pl.when(has_right)
        def _():
            own_copy(2, here + 1, piece).wait_send()

    @pl.loop(0, count)
    def _(slot):
        sent = ((slot < here) & has_right) | ((slot > here) & has_left)

        @pl.when(sent)
        def _():
            for piece in range(PARTS):
                pass_copy(slot, here, piece).wait_send()


def write_out(flow_in, matched_in, flow, matched, flow_sem, matched_sem):
    flow_copy = pltpu.make_async_copy(flow_in, flow, flow_sem)
    matched_copy = pltpu.make_async_copy(matched_in, matched, matched_sem)
    matched_copy.start()
    flow_copy.start()
    matched_copy.wait()
    flow_copy.wait()


def body(count, features):
    rows, chans = features.shape[2], features.shape[3]
    shapes = (
        jax.ShapeDtypeStruct((1, 1, 2, rows), jnp.float32),
        jax.ShapeDtypeStruct((1, 1, rows, chans), jnp.bfloat16),
    )
    flow, matched = pl.pallas_call(
        functools.partial(kernel, count),
        out_shape=shapes,
        in_specs=[pl.BlockSpec(memory_space=pl.ANY)],
        out_specs=(
            pl.BlockSpec(memory_space=pltpu.VMEM),
            pl.BlockSpec(memory_space=pltpu.VMEM),
        ),
        scratch_shapes=[
            pltpu.VMEM((rows, chans), jnp.bfloat16),
            pltpu.VMEM((count, rows, chans), jnp.bfloat16),
            pltpu.VMEM((count, SUMS, rows), jnp.bfloat16),
            pltpu.VMEM((1, rows), jnp.float32),
            pltpu.VMEM((chans + SUMS, rows), jnp.float32),
            pltpu.SemaphoreType.DMA((3, PARTS)),
            pltpu.SemaphoreType.DMA((count, PARTS)),
            pltpu.SemaphoreType.DMA((count, PARTS)),
            pltpu.SemaphoreType.DMA,
        ],
        compiler_params=pltpu.CompilerParams(
            collective_id=0, has_side_effects=True, vmem_limit_bytes=LIMIT
        ),
    )(features)
    return pl.pallas_call(
        write_out,
        out_shape=shapes,
        in_specs=[pl.BlockSpec(memory_space=pl.ANY)] * 2,
        out_specs=[pl.BlockSpec(memory_space=pl.ANY)] * 2,
        scratch_shapes=[pltpu.SemaphoreType.DMA, pltpu.SemaphoreType.DMA],
        compiler_params=pltpu.CompilerParams(vmem_limit_bytes=2**20),
    )(flow, matched)


def solution(mesh):
    placed = (P(("clips", "pair"), "dir", "pix", None),)
    return jax.shard_map(
        functools.partial(body, mesh.shape["pix"]),
        mesh=mesh,
        in_specs=placed,
        out_specs=(
            P(("clips", "pair"), "dir", None, "pix"),
            P(("clips", "pair"), "dir", "pix", None),
        ),
        check_vma=False,
    )
```

```python
import functools
import math

import jax
import jax.numpy as jnp
from jax import lax
from jax.experimental import pallas as pl
from jax.experimental.pallas import tpu as pltpu
from jax.sharding import PartitionSpec as P

W = 120
LOWEST = -1e30
PARTS = 2
WIDTH = 512
SUMS = 16
LIMIT = 55056 * 2**10
MESH = pl.DeviceIdType.MESH


def grid_position(index):
    row = jnp.floor((index + 0.5) * (1.0 / W))
    return index - row * W, row


def kernel(
    count, feats, flow, matched, queries, held, places, top, acc, own_sem, pass_sem, recv_sem, load_sem
):
    rows, chans = feats.shape[2], feats.shape[3]
    part = rows // PARTS
    scale = math.log2(math.e) / math.sqrt(chans)
    here = lax.axis_index("pix")
    side = lax.axis_index("dir")
    other = 1 - side
    has_left = here > 0
    has_right = here < count - 1

    load = pltpu.make_async_copy(feats.at[0, 0], queries, load_sem)
    load.start()

    barrier = pltpu.get_barrier_semaphore()

    def greet(pix, core):
        pl.semaphore_signal(
            barrier, inc=1, device_id={"pix": pix, "dir": core}, device_id_type=MESH
        )

    greet(here, other)

    @pl.when(has_left)
    def _():
        greet(here - 1, other)
        greet(here - 1, side)

    @pl.when(has_right)
    def _():
        greet(here + 1, other)
        greet(here + 1, side)

    neighbours = has_left.astype(jnp.int32) + has_right.astype(jnp.int32)
    pl.semaphore_wait(barrier, 1 + 2 * neighbours)

    def own_copy(which, pix, piece):
        span = pl.ds(piece * part, part)
        return pltpu.make_async_remote_copy(
            src_ref=feats.at[0, 0, span],
            dst_ref=held.at[here, span],
            send_sem=own_sem.at[which, piece],
            recv_sem=recv_sem.at[here, piece],
            device_id={"pix": pix, "dir": other},
            device_id_type=MESH,
        )

    def pass_copy(slot, pix, piece):
        span = pl.ds(piece * part, part)
        return pltpu.make_async_remote_copy(
            src_ref=held.at[slot, span],
            dst_ref=held.at[slot, span],
            send_sem=pass_sem.at[slot, piece],
            recv_sem=recv_sem.at[slot, piece],
            device_id={"pix": pix, "dir": side},
            device_id_type=MESH,
        )

    for piece in range(PARTS):

        @pl.when(has_left)
        def _():
            own_copy(1, here - 1, piece).start()

        @pl.when(has_right)
        def _():
            own_copy(2, here + 1, piece).start()

    for piece in range(PARTS):
        own_copy(0, here, piece).start()

    line = lax.broadcasted_iota(jnp.int32, (SUMS, rows), 0)
    local = lax.broadcasted_iota(jnp.int32, (SUMS, rows), 1)

    @pl.loop(0, count)
    def _(slot):
        col, row = grid_position((local + slot * rows).astype(jnp.float32))
        tags = jnp.where(line == 0, 1.0, jnp.where(line == 1, col, jnp.where(line == 2, row, 0.0)))
        places[slot] = tags.astype(jnp.bfloat16)

    top[...] = jnp.full_like(top, LOWEST)
    acc[...] = jnp.zeros_like(acc)
    load.wait()

    short = jnp.minimum(here, count - 1 - here)
    long_left = here > count - 1 - here

    def slot_of(item):
        paired = item <= 2 * short
        step = jnp.where(paired, (item + 1) // 2, item - short)
        left = jnp.where(paired, item % 2 == 1, long_left)
        return jnp.where(left, here - step, here + step)

    def arrive(slot, piece):
        pass_copy(slot, here, piece).wait_recv()

        @pl.when((slot < here) & has_right)
        def _():
            pass_copy(slot, here + 1, piece).start()

        @pl.when((slot > here) & has_left)
        def _():
            pass_copy(slot, here - 1, piece).start()

    def fold(slot, first, length):
        keys = held[slot, first : first + length]
        values = jnp.concatenate([keys.T, places[slot, :, first : first + length]], axis=0)
        for start in range(0, rows, WIDTH):
            some = slice(start, min(start + WIDTH, rows))
            scores = lax.dot_general(
                keys, queries[some], (((1,), (1,)), ((), ())), preferred_element_type=jnp.float32
            )
            old = top[:, some]
            new = jnp.maximum(old, jnp.max(scores, axis=0, keepdims=True))
            fade = jnp.exp2((old - new) * scale)
            weights = jnp.exp2((scores - new) * scale).astype(jnp.bfloat16)
            top[:, some] = new
            acc[:, some] = acc[:, some] * fade + jnp.dot(
                values, weights, preferred_element_type=jnp.float32
            )

    @pl.loop(0, count - 1)
    def _(item):
        slot = slot_of(item)
        opens = (item % 2 == 1) & (item < 2 * short)
        second = (item > 0) & (item % 2 == 0) & (item <= 2 * short)
        for piece in range(PARTS):

            @pl.when(jnp.logical_not(second))
            def _():
                arrive(slot, piece)

            @pl.when(opens)
            def _():
                arrive(slot_of(item + 1), piece)

        fold(slot, 0, rows)

    final = slot_of(count - 1)
    for piece in range(PARTS):

        @pl.when((here == 0) | (here == count - 1) | (count > 2 * short + 1))
        def _():
            arrive(final, piece)

        fold(final, piece * part, part)

    inverse = 1.0 / acc[chans : chans + 1]
    matched[0, 0] = (acc[:chans] * inverse).T.astype(matched.dtype)
    means = acc[chans : chans + 8] * inverse
    index = (lax.broadcasted_iota(jnp.int32, (1, rows), 1) + here * rows).astype(jnp.float32)
    col, row = grid_position(index)
    flow[0, 0, 0:1] = (means[1:2] - col) * (1.0 / W)
    flow[0, 0, 1:2] = (means[2:3] - row) * (1.0 / W)

    for piece in range(PARTS):
        own_copy(0, here, piece).wait_send()

        @pl.when(has_left)
        def _():
            own_copy(1, here - 1, piece).wait_send()

        @pl.when(has_right)
        def _():
            own_copy(2, here + 1, piece).wait_send()

    @pl.loop(0, count)
    def _(slot):
        sent = ((slot < here) & has_right) | ((slot > here) & has_left)

        @pl.when(sent)
        def _():
            for piece in range(PARTS):
                pass_copy(slot, here, piece).wait_send()


def write_out(flow_in, matched_in, flow, matched, flow_sem, matched_sem):
    flow_copy = pltpu.make_async_copy(flow_in, flow, flow_sem)
    matched_copy = pltpu.make_async_copy(matched_in, matched, matched_sem)
    matched_copy.start()
    flow_copy.start()
    matched_copy.wait()
    flow_copy.wait()


def body(count, features):
    rows, chans = features.shape[2], features.shape[3]
    shapes = (
        jax.ShapeDtypeStruct((1, 1, 2, rows), jnp.float32),
        jax.ShapeDtypeStruct((1, 1, rows, chans), jnp.bfloat16),
    )
    flow, matched = pl.pallas_call(
        functools.partial(kernel, count),
        out_shape=shapes,
        in_specs=[pl.BlockSpec(memory_space=pl.ANY)],
        out_specs=(
            pl.BlockSpec(memory_space=pltpu.VMEM),
            pl.BlockSpec(memory_space=pltpu.VMEM),
        ),
        scratch_shapes=[
            pltpu.VMEM((rows, chans), jnp.bfloat16),
            pltpu.VMEM((count, rows, chans), jnp.bfloat16),
            pltpu.VMEM((count, SUMS, rows), jnp.bfloat16),
            pltpu.VMEM((1, rows), jnp.float32),
            pltpu.VMEM((chans + SUMS, rows), jnp.float32),
            pltpu.SemaphoreType.DMA((3, PARTS)),
            pltpu.SemaphoreType.DMA((count, PARTS)),
            pltpu.SemaphoreType.DMA((count, PARTS)),
            pltpu.SemaphoreType.DMA,
        ],
        compiler_params=pltpu.CompilerParams(
            collective_id=0, has_side_effects=True, vmem_limit_bytes=LIMIT
        ),
    )(features)
    return pl.pallas_call(
        write_out,
        out_shape=shapes,
        in_specs=[pl.BlockSpec(memory_space=pl.ANY)] * 2,
        out_specs=[pl.BlockSpec(memory_space=pl.ANY)] * 2,
        scratch_shapes=[pltpu.SemaphoreType.DMA, pltpu.SemaphoreType.DMA],
        compiler_params=pltpu.CompilerParams(vmem_limit_bytes=2**20),
    )(flow, matched)


def solution(mesh):
    placed = (P(("clips", "pair"), "dir", "pix", None),)
    return jax.shard_map(
        functools.partial(body, mesh.shape["pix"]),
        mesh=mesh,
        in_specs=placed,
        out_specs=(
            P(("clips", "pair"), "dir", None, "pix"),
            P(("clips", "pair"), "dir", "pix", None),
        ),
        check_vma=False,
    )
```

```python
import functools
import math

import jax
import jax.numpy as jnp
from jax import lax
from jax.experimental import pallas as pl
from jax.experimental.pallas import tpu as pltpu
from jax.sharding import PartitionSpec as P

W = 120
LOWEST = -1e30
PARTS = 3
WIDTH = 512
SUMS = 16
LIMIT = 55056 * 2**10
MESH = pl.DeviceIdType.MESH


def grid_position(index):
    row = jnp.floor((index + 0.5) * (1.0 / W))
    return index - row * W, row


def kernel(
    count, feats, flow, matched, queries, held, places, top, acc, own_sem, pass_sem, recv_sem, load_sem, ready
):
    rows, chans = feats.shape[2], feats.shape[3]
    part = rows // PARTS
    scale = math.log2(math.e) / math.sqrt(chans)
    here = lax.axis_index("pix")
    side = lax.axis_index("dir")
    other = 1 - side
    has_left = here > 0
    has_right = here < count - 1

    load = pltpu.make_async_copy(feats.at[0, 0], queries, load_sem)
    load.start()

    barrier = pltpu.get_barrier_semaphore()

    def greet(sem, pix, core):
        pl.semaphore_signal(
            sem, inc=1, device_id={"pix": pix, "dir": core}, device_id_type=MESH
        )

    greet(barrier, here, other)

    @pl.when(has_right)
    def _():
        greet(barrier, here + 1, other)
        greet(barrier, here + 1, side)

    pl.semaphore_wait(barrier, 1 + 2 * has_left.astype(jnp.int32))

    def own_copy(which, pix, piece):
        span = pl.ds(piece * part, part)
        return pltpu.make_async_remote_copy(
            src_ref=feats.at[0, 0, span],
            dst_ref=held.at[here, span],
            send_sem=own_sem.at[which, piece],
            recv_sem=recv_sem.at[here, piece],
            device_id={"pix": pix, "dir": other},
            device_id_type=MESH,
        )

    def pass_copy(slot, pix, piece):
        span = pl.ds(piece * part, part)
        return pltpu.make_async_remote_copy(
            src_ref=held.at[slot, span],
            dst_ref=held.at[slot, span],
            send_sem=pass_sem.at[slot, piece],
            recv_sem=recv_sem.at[slot, piece],
            device_id={"pix": pix, "dir": side},
            device_id_type=MESH,
        )

    @pl.when(has_left)
    def _():
        greet(ready, here - 1, other)
        greet(ready, here - 1, side)
        for piece in range(PARTS):
            own_copy(1, here - 1, piece).start()

    for piece in range(PARTS):
        own_copy(0, here, piece).start()

    @pl.when(has_right)
    def _():
        pl.semaphore_wait(ready, 2)
        for piece in range(PARTS):
            own_copy(2, here + 1, piece).start()

    line = lax.broadcasted_iota(jnp.int32, (SUMS, rows), 0)
    local = lax.broadcasted_iota(jnp.int32, (SUMS, rows), 1)

    @pl.loop(0, count)
    def _(slot):
        col, row = grid_position((local + slot * rows).astype(jnp.float32))
        tags = jnp.where(line == 0, 1.0, jnp.where(line == 1, col, jnp.where(line == 2, row, 0.0)))
        places[slot] = tags.astype(jnp.bfloat16)

    top[...] = jnp.full_like(top, LOWEST)
    acc[...] = jnp.zeros_like(acc)
    load.wait()

    short = jnp.minimum(here, count - 1 - here)
    long_left = here > count - 1 - here

    def slot_of(item):
        paired = item <= 2 * short
        step = jnp.where(paired, (item + 1) // 2, item - short)
        left = jnp.where(paired, item % 2 == 1, long_left)
        return jnp.where(left, here - step, here + step)

    def arrive(slot, piece):
        pass_copy(slot, here, piece).wait_recv()

        @pl.when((slot < here) & has_right)
        def _():
            pass_copy(slot, here + 1, piece).start()

        @pl.when((slot > here) & has_left)
        def _():
            pass_copy(slot, here - 1, piece).start()

    def fold(slot, first, length):
        keys = held[slot, first : first + length]
        values = jnp.concatenate([keys.T, places[slot, :, first : first + length]], axis=0)
        for start in range(0, rows, WIDTH):
            some = slice(start, min(start + WIDTH, rows))
            scores = lax.dot_general(
                keys, queries[some], (((1,), (1,)), ((), ())), preferred_element_type=jnp.float32
            )
            old = top[:, some]
            new = jnp.maximum(old, jnp.max(scores, axis=0, keepdims=True))
            fade = jnp.exp2((old - new) * scale)
            weights = jnp.exp2((scores - new) * scale).astype(jnp.bfloat16)
            top[:, some] = new
            acc[:, some] = acc[:, some] * fade + jnp.dot(
                values, weights, preferred_element_type=jnp.float32
            )

    @pl.loop(0, count - 1)
    def _(item):
        slot = slot_of(item)
        opens = (item % 2 == 1) & (item < 2 * short)
        second = (item > 0) & (item % 2 == 0) & (item <= 2 * short)
        for piece in range(PARTS):

            @pl.when(jnp.logical_not(second))
            def _():
                arrive(slot, piece)

            @pl.when(opens)
            def _():
                arrive(slot_of(item + 1), piece)

        fold(slot, 0, rows)

    final = slot_of(count - 1)
    for piece in range(PARTS):

        @pl.when((here == 0) | (here == count - 1) | (count > 2 * short + 1))
        def _():
            arrive(final, piece)

        fold(final, piece * part, part)

    inverse = 1.0 / acc[chans : chans + 1]
    matched[0, 0] = (acc[:chans] * inverse).T.astype(matched.dtype)
    means = acc[chans : chans + 8] * inverse
    index = (lax.broadcasted_iota(jnp.int32, (1, rows), 1) + here * rows).astype(jnp.float32)
    col, row = grid_position(index)
    flow[0, 0, 0:1] = (means[1:2] - col) * (1.0 / W)
    flow[0, 0, 1:2] = (means[2:3] - row) * (1.0 / W)

    for piece in range(PARTS):
        own_copy(0, here, piece).wait_send()

        @pl.when(has_left)
        def _():
            own_copy(1, here - 1, piece).wait_send()

        @pl.when(has_right)
        def _():
            own_copy(2, here + 1, piece).wait_send()

    @pl.loop(0, count)
    def _(slot):
        sent = ((slot < here) & has_right) | ((slot > here) & has_left)

        @pl.when(sent)
        def _():
            for piece in range(PARTS):
                pass_copy(slot, here, piece).wait_send()


def write_out(flow_in, matched_in, flow, matched, flow_sem, matched_sem):
    flow_copy = pltpu.make_async_copy(flow_in, flow, flow_sem)
    matched_copy = pltpu.make_async_copy(matched_in, matched, matched_sem)
    matched_copy.start()
    flow_copy.start()
    matched_copy.wait()
    flow_copy.wait()


def body(count, features):
    rows, chans = features.shape[2], features.shape[3]
    shapes = (
        jax.ShapeDtypeStruct((1, 1, 2, rows), jnp.float32),
        jax.ShapeDtypeStruct((1, 1, rows, chans), jnp.bfloat16),
    )
    flow, matched = pl.pallas_call(
        functools.partial(kernel, count),
        out_shape=shapes,
        in_specs=[pl.BlockSpec(memory_space=pl.ANY)],
        out_specs=(
            pl.BlockSpec(memory_space=pltpu.VMEM),
            pl.BlockSpec(memory_space=pltpu.VMEM),
        ),
        scratch_shapes=[
            pltpu.VMEM((rows, chans), jnp.bfloat16),
            pltpu.VMEM((count, rows, chans), jnp.bfloat16),
            pltpu.VMEM((count, SUMS, rows), jnp.bfloat16),
            pltpu.VMEM((1, rows), jnp.float32),
            pltpu.VMEM((chans + SUMS, rows), jnp.float32),
            pltpu.SemaphoreType.DMA((3, PARTS)),
            pltpu.SemaphoreType.DMA((count, PARTS)),
            pltpu.SemaphoreType.DMA((count, PARTS)),
            pltpu.SemaphoreType.DMA,
            pltpu.SemaphoreType.REGULAR,
        ],
        compiler_params=pltpu.CompilerParams(
            collective_id=0, has_side_effects=True, vmem_limit_bytes=LIMIT
        ),
    )(features)
    return pl.pallas_call(
        write_out,
        out_shape=shapes,
        in_specs=[pl.BlockSpec(memory_space=pl.ANY)] * 2,
        out_specs=[pl.BlockSpec(memory_space=pl.ANY)] * 2,
        scratch_shapes=[pltpu.SemaphoreType.DMA, pltpu.SemaphoreType.DMA],
        compiler_params=pltpu.CompilerParams(vmem_limit_bytes=2**20),
    )(flow, matched)


def solution(mesh):
    placed = (P(("clips", "pair"), "dir", "pix", None),)
    return jax.shard_map(
        functools.partial(body, mesh.shape["pix"]),
        mesh=mesh,
        in_specs=placed,
        out_specs=(
            P(("clips", "pair"), "dir", None, "pix"),
            P(("clips", "pair"), "dir", "pix", None),
        ),
        check_vma=False,
    )
```

```python
import functools
import math

import jax
import jax.numpy as jnp
from jax import lax
from jax.experimental import pallas as pl
from jax.experimental.pallas import tpu as pltpu
from jax.sharding import PartitionSpec as P

W = 120
LOWEST = -1e30
PARTS = 3
WIDTH = 512
SUMS = 16
LIMIT = 55056 * 2**10
MESH = pl.DeviceIdType.MESH


def grid_position(index):
    row = jnp.floor((index + 0.5) * (1.0 / W))
    return index - row * W, row


def kernel(
    count, feats, flow, matched, queries, held, places, top, acc, own_sem, pass_sem, recv_sem, load_sem
):
    rows, chans = feats.shape[2], feats.shape[3]
    part = rows // PARTS
    scale = math.log2(math.e) / math.sqrt(chans)
    here = lax.axis_index("pix")
    side = lax.axis_index("dir")
    other = 1 - side
    has_left = here > 0
    has_right = here < count - 1

    load = pltpu.make_async_copy(feats.at[0, 0], queries, load_sem)
    load.start()

    barrier = pltpu.get_barrier_semaphore()

    def greet(pix, core):
        pl.semaphore_signal(
            barrier, inc=1, device_id={"pix": pix, "dir": core}, device_id_type=MESH
        )

    greet(here, other)

    @pl.when(has_left)
    def _():
        greet(here - 1, other)
        greet(here - 1, side)

    @pl.when(has_right)
    def _():
        greet(here + 1, other)
        greet(here + 1, side)

    neighbours = has_left.astype(jnp.int32) + has_right.astype(jnp.int32)
    pl.semaphore_wait(barrier, 1 + 2 * neighbours)

    def own_copy(which, pix, piece):
        span = pl.ds(piece * part, part)
        return pltpu.make_async_remote_copy(
            src_ref=feats.at[0, 0, span],
            dst_ref=held.at[here, span],
            send_sem=own_sem.at[which, piece],
            recv_sem=recv_sem.at[here, piece],
            device_id={"pix": pix, "dir": other},
            device_id_type=MESH,
        )

    def pass_copy(slot, pix, piece):
        span = pl.ds(piece * part, part)
        return pltpu.make_async_remote_copy(
            src_ref=held.at[slot, span],
            dst_ref=held.at[slot, span],
            send_sem=pass_sem.at[slot, piece],
            recv_sem=recv_sem.at[slot, piece],
            device_id={"pix": pix, "dir": side},
            device_id_type=MESH,
        )

    for piece in range(PARTS):

        @pl.when(has_left)
        def _():
            own_copy(1, here - 1, piece).start()

        @pl.when(has_right)
        def _():
            own_copy(2, here + 1, piece).start()

    for piece in range(PARTS):
        own_copy(0, here, piece).start()

    line = lax.broadcasted_iota(jnp.int32, (SUMS, rows), 0)
    local = lax.broadcasted_iota(jnp.int32, (SUMS, rows), 1)

    @pl.loop(0, count)
    def _(slot):
        col, row = grid_position((local + slot * rows).astype(jnp.float32))
        tags = jnp.where(line == 0, 1.0, jnp.where(line == 1, col, jnp.where(line == 2, row, 0.0)))
        places[slot] = tags.astype(jnp.bfloat16)

    top[...] = jnp.full_like(top, LOWEST)
    acc[...] = jnp.zeros_like(acc)
    load.wait()

    short = jnp.minimum(here, count - 1 - here)
    long_left = here > count - 1 - here

    def slot_of(item):
        paired = item <= 2 * short
        step = jnp.where(paired, (item + 1) // 2, item - short)
        left = jnp.where(paired, item % 2 == 1, long_left)
        return jnp.where(left, here - step, here + step)

    def arrive(slot, piece):
        pass_copy(slot, here, piece).wait_recv()

        @pl.when((slot < here) & has_right)
        def _():
            pass_copy(slot, here + 1, piece).start()

        @pl.when((slot > here) & has_left)
        def _():
            pass_copy(slot, here - 1, piece).start()

    def fold(slot, first, length):
        keys = held[slot, first : first + length]
        values = jnp.concatenate([keys.T, places[slot, :, first : first + length]], axis=0)
        for start in range(0, rows, WIDTH):
            some = slice(start, min(start + WIDTH, rows))
            scores = lax.dot_general(
                keys, queries[some], (((1,), (1,)), ((), ())), preferred_element_type=jnp.float32
            )
            old = top[:, some]
            new = jnp.maximum(old, jnp.max(scores, axis=0, keepdims=True))
            fade = jnp.exp2((old - new) * scale)
            weights = jnp.exp2((scores - new) * scale).astype(jnp.bfloat16)
            top[:, some] = new
            acc[:, some] = acc[:, some] * fade + jnp.dot(
                values, weights, preferred_element_type=jnp.float32
            )

    @pl.loop(0, count - 1)
    def _(item):
        slot = slot_of(item)
        opens = (item % 2 == 1) & (item < 2 * short)
        second = (item > 0) & (item % 2 == 0) & (item <= 2 * short)
        for piece in range(PARTS):

            @pl.when(jnp.logical_not(second))
            def _():
                arrive(slot, piece)

            @pl.when(opens)
            def _():
                arrive(slot_of(item + 1), piece)

        fold(slot, 0, rows)

    final = slot_of(count - 1)
    for piece in range(PARTS):

        @pl.when((here == 0) | (here == count - 1) | (count > 2 * short + 1))
        def _():
            arrive(final, piece)

        fold(final, piece * part, part)

    inverse = 1.0 / acc[chans : chans + 1]
    matched[0, 0] = (acc[:chans] * inverse).T.astype(matched.dtype)
    means = acc[chans : chans + 8] * inverse
    index = (lax.broadcasted_iota(jnp.int32, (1, rows), 1) + here * rows).astype(jnp.float32)
    col, row = grid_position(index)
    flow[0, 0, 0:1] = (means[1:2] - col) * (1.0 / W)
    flow[0, 0, 1:2] = (means[2:3] - row) * (1.0 / W)

    for piece in range(PARTS):
        own_copy(0, here, piece).wait_send()

        @pl.when(has_left)
        def _():
            own_copy(1, here - 1, piece).wait_send()

        @pl.when(has_right)
        def _():
            own_copy(2, here + 1, piece).wait_send()

    @pl.loop(0, count)
    def _(slot):
        sent = ((slot < here) & has_right) | ((slot > here) & has_left)

        @pl.when(sent)
        def _():
            for piece in range(PARTS):
                pass_copy(slot, here, piece).wait_send()


def write_out(flow_in, matched_in, flow, matched, flow_sem, matched_sem):
    flow_copy = pltpu.make_async_copy(flow_in, flow, flow_sem)
    matched_copy = pltpu.make_async_copy(matched_in, matched, matched_sem)
    matched_copy.start()
    flow_copy.start()
    matched_copy.wait()
    flow_copy.wait()


def body(count, features):
    rows, chans = features.shape[2], features.shape[3]
    shapes = (
        jax.ShapeDtypeStruct((1, 1, 2, rows), jnp.float32),
        jax.ShapeDtypeStruct((1, 1, rows, chans), jnp.bfloat16),
    )
    flow, matched = pl.pallas_call(
        functools.partial(kernel, count),
        out_shape=shapes,
        in_specs=[pl.BlockSpec(memory_space=pl.ANY)],
        out_specs=(
            pl.BlockSpec(memory_space=pltpu.VMEM),
            pl.BlockSpec(memory_space=pltpu.VMEM),
        ),
        scratch_shapes=[
            pltpu.VMEM((rows, chans), jnp.bfloat16),
            pltpu.VMEM((count, rows, chans), jnp.bfloat16),
            pltpu.VMEM((count, SUMS, rows), jnp.bfloat16),
            pltpu.VMEM((1, rows), jnp.float32),
            pltpu.VMEM((chans + SUMS, rows), jnp.float32),
            pltpu.SemaphoreType.DMA((3, PARTS)),
            pltpu.SemaphoreType.DMA((count, PARTS)),
            pltpu.SemaphoreType.DMA((count, PARTS)),
            pltpu.SemaphoreType.DMA,
        ],
        compiler_params=pltpu.CompilerParams(
            collective_id=0, has_side_effects=True, vmem_limit_bytes=LIMIT
        ),
    )(features)
    return pl.pallas_call(
        write_out,
        out_shape=shapes,
        in_specs=[pl.BlockSpec(memory_space=pl.ANY)] * 2,
        out_specs=[pl.BlockSpec(memory_space=pl.ANY)] * 2,
        scratch_shapes=[pltpu.SemaphoreType.DMA, pltpu.SemaphoreType.DMA],
        compiler_params=pltpu.CompilerParams(vmem_limit_bytes=2**20),
    )(flow, matched)


def solution(mesh):
    placed = (P(("clips", "pair"), "dir", "pix", None),)
    return jax.shard_map(
        functools.partial(body, mesh.shape["pix"]),
        mesh=mesh,
        in_specs=placed,
        out_specs=(
            P(("clips", "pair"), "dir", None, "pix"),
            P(("clips", "pair"), "dir", "pix", None),
        ),
        check_vma=False,
    )
```

```python
import functools
import math

import jax
import jax.numpy as jnp
from jax import lax
from jax.experimental import pallas as pl
from jax.experimental.pallas import tpu as pltpu
from jax.sharding import PartitionSpec as P

W = 120
LOWEST = -1e30
PARTS = 3
WIDTH = 512
SUMS = 16
LIMIT = 55056 * 2**10
MESH = pl.DeviceIdType.MESH


def grid_position(index):
    row = jnp.floor((index + 0.5) * (1.0 / W))
    return index - row * W, row


def kernel(
    count, feats, flow, matched, queries, held, places, top, acc, own_sem, pass_sem, recv_sem, load_sem
):
    rows, chans = feats.shape[2], feats.shape[3]
    part = rows // PARTS
    scale = math.log2(math.e) / math.sqrt(chans)
    here = lax.axis_index("pix")
    side = lax.axis_index("dir")
    other = 1 - side
    has_left = here > 0
    has_right = here < count - 1

    load = pltpu.make_async_copy(feats.at[0, 0], queries, load_sem)
    load.start()

    barrier = pltpu.get_barrier_semaphore()

    def greet(pix, core):
        pl.semaphore_signal(
            barrier, inc=1, device_id={"pix": pix, "dir": core}, device_id_type=MESH
        )

    greet(here, other)

    @pl.when(has_left)
    def _():
        greet(here - 1, other)
        greet(here - 1, side)

    @pl.when(has_right)
    def _():
        greet(here + 1, other)
        greet(here + 1, side)

    neighbours = has_left.astype(jnp.int32) + has_right.astype(jnp.int32)
    pl.semaphore_wait(barrier, 1 + 2 * neighbours)

    def own_copy(which, pix, piece):
        span = pl.ds(piece * part, part)
        return pltpu.make_async_remote_copy(
            src_ref=feats.at[0, 0, span],
            dst_ref=held.at[here, span],
            send_sem=own_sem.at[which, piece],
            recv_sem=recv_sem.at[here, piece],
            device_id={"pix": pix, "dir": other},
            device_id_type=MESH,
        )

    def pass_copy(slot, pix, piece):
        span = pl.ds(piece * part, part)
        return pltpu.make_async_remote_copy(
            src_ref=held.at[slot, span],
            dst_ref=held.at[slot, span],
            send_sem=pass_sem.at[slot, piece],
            recv_sem=recv_sem.at[slot, piece],
            device_id={"pix": pix, "dir": side},
            device_id_type=MESH,
        )

    for piece in range(PARTS):

        @pl.when(has_left)
        def _():
            own_copy(1, here - 1, piece).start()

    for piece in range(PARTS):

        @pl.when(has_right)
        def _():
            own_copy(2, here + 1, piece).start()

    for piece in range(PARTS):
        own_copy(0, here, piece).start()

    line = lax.broadcasted_iota(jnp.int32, (SUMS, rows), 0)
    local = lax.broadcasted_iota(jnp.int32, (SUMS, rows), 1)

    @pl.loop(0, count)
    def _(slot):
        col, row = grid_position((local + slot * rows).astype(jnp.float32))
        tags = jnp.where(line == 0, 1.0, jnp.where(line == 1, col, jnp.where(line == 2, row, 0.0)))
        places[slot] = tags.astype(jnp.bfloat16)

    top[...] = jnp.full_like(top, LOWEST)
    acc[...] = jnp.zeros_like(acc)
    load.wait()

    short = jnp.minimum(here, count - 1 - here)
    long_left = here > count - 1 - here

    def slot_of(item):
        paired = item <= 2 * short
        step = jnp.where(paired, (item + 1) // 2, item - short)
        left = jnp.where(paired, item % 2 == 1, long_left)
        return jnp.where(left, here - step, here + step)

    def arrive(slot, piece):
        pass_copy(slot, here, piece).wait_recv()

        @pl.when((slot < here) & has_right)
        def _():
            pass_copy(slot, here + 1, piece).start()

        @pl.when((slot > here) & has_left)
        def _():
            pass_copy(slot, here - 1, piece).start()

    def fold(slot, first, length):
        keys = held[slot, first : first + length]
        values = jnp.concatenate([keys.T, places[slot, :, first : first + length]], axis=0)
        for start in range(0, rows, WIDTH):
            some = slice(start, min(start + WIDTH, rows))
            scores = lax.dot_general(
                keys, queries[some], (((1,), (1,)), ((), ())), preferred_element_type=jnp.float32
            )
            old = top[:, some]
            new = jnp.maximum(old, jnp.max(scores, axis=0, keepdims=True))
            fade = jnp.exp2((old - new) * scale)
            weights = jnp.exp2((scores - new) * scale).astype(jnp.bfloat16)
            top[:, some] = new
            acc[:, some] = acc[:, some] * fade + jnp.dot(
                values, weights, preferred_element_type=jnp.float32
            )

    @pl.loop(0, count - 1)
    def _(item):
        slot = slot_of(item)
        opens = (item % 2 == 1) & (item < 2 * short)
        second = (item > 0) & (item % 2 == 0) & (item <= 2 * short)
        for piece in range(PARTS):

            @pl.when(jnp.logical_not(second))
            def _():
                arrive(slot, piece)

            @pl.when(opens)
            def _():
                arrive(slot_of(item + 1), piece)

        fold(slot, 0, rows)

    final = slot_of(count - 1)
    for piece in range(PARTS):

        @pl.when((here == 0) | (here == count - 1) | (count > 2 * short + 1))
        def _():
            arrive(final, piece)

        fold(final, piece * part, part)

    inverse = 1.0 / acc[chans : chans + 1]
    matched[0, 0] = (acc[:chans] * inverse).astype(matched.dtype).T
    means = acc[chans : chans + 8] * inverse
    index = (lax.broadcasted_iota(jnp.int32, (1, rows), 1) + here * rows).astype(jnp.float32)
    col, row = grid_position(index)
    flow[0, 0, 0:1] = (means[1:2] - col) * (1.0 / W)
    flow[0, 0, 1:2] = (means[2:3] - row) * (1.0 / W)

    for piece in range(PARTS):
        own_copy(0, here, piece).wait_send()

        @pl.when(has_left)
        def _():
            own_copy(1, here - 1, piece).wait_send()

        @pl.when(has_right)
        def _():
            own_copy(2, here + 1, piece).wait_send()

    @pl.loop(0, count)
    def _(slot):
        sent = ((slot < here) & has_right) | ((slot > here) & has_left)

        @pl.when(sent)
        def _():
            for piece in range(PARTS):
                pass_copy(slot, here, piece).wait_send()


def write_out(flow_in, matched_in, flow, matched, flow_sem, matched_sem):
    flow_copy = pltpu.make_async_copy(flow_in, flow, flow_sem)
    matched_copy = pltpu.make_async_copy(matched_in, matched, matched_sem)
    matched_copy.start()
    flow_copy.start()
    matched_copy.wait()
    flow_copy.wait()


def body(count, features):
    rows, chans = features.shape[2], features.shape[3]
    shapes = (
        jax.ShapeDtypeStruct((1, 1, 2, rows), jnp.float32),
        jax.ShapeDtypeStruct((1, 1, rows, chans), jnp.bfloat16),
    )
    flow, matched = pl.pallas_call(
        functools.partial(kernel, count),
        out_shape=shapes,
        in_specs=[pl.BlockSpec(memory_space=pl.ANY)],
        out_specs=(
            pl.BlockSpec(memory_space=pltpu.VMEM),
            pl.BlockSpec(memory_space=pltpu.VMEM),
        ),
        scratch_shapes=[
            pltpu.VMEM((rows, chans), jnp.bfloat16),
            pltpu.VMEM((count, rows, chans), jnp.bfloat16),
            pltpu.VMEM((count, SUMS, rows), jnp.bfloat16),
            pltpu.VMEM((1, rows), jnp.float32),
            pltpu.VMEM((chans + SUMS, rows), jnp.float32),
            pltpu.SemaphoreType.DMA((3, PARTS)),
            pltpu.SemaphoreType.DMA((count, PARTS)),
            pltpu.SemaphoreType.DMA((count, PARTS)),
            pltpu.SemaphoreType.DMA,
        ],
        compiler_params=pltpu.CompilerParams(
            collective_id=0, has_side_effects=True, vmem_limit_bytes=LIMIT
        ),
    )(features)
    return pl.pallas_call(
        write_out,
        out_shape=shapes,
        in_specs=[pl.BlockSpec(memory_space=pl.ANY)] * 2,
        out_specs=[pl.BlockSpec(memory_space=pl.ANY)] * 2,
        scratch_shapes=[pltpu.SemaphoreType.DMA, pltpu.SemaphoreType.DMA],
        compiler_params=pltpu.CompilerParams(vmem_limit_bytes=2**20),
    )(flow, matched)


def solution(mesh):
    placed = (P(("clips", "pair"), "dir", "pix", None),)
    return jax.shard_map(
        functools.partial(body, mesh.shape["pix"]),
        mesh=mesh,
        in_specs=placed,
        out_specs=(
            P(("clips", "pair"), "dir", None, "pix"),
            P(("clips", "pair"), "dir", "pix", None),
        ),
        check_vma=False,
    )
```
